32 devices in a mesh: groups: 2 (over y), tensor: 4 (over z), dp: 4 (over x, core).
Axes of the slice: x: 2, y: 2, z: 4, core: 2. Of those that a mesh axis runs over, the one named last changes fastest.
Arguments:
- tokens: bfloat16 [1024, 8192], P(('groups', 'dp'), 'tensor'), parts along dimension 0, may hold values from -6 to 6
- in_weight: bfloat16 [8192, 2, 8192], P('dp', None, 'tensor'), may hold values from -0.0625 to 0.0625
- conv_weight: float32 [4, 8192], P(None, 'tensor'), may hold values from -3 to 3
- conv_bias: float32 [8192], P('tensor'), may hold values from -3 to 3
- conv_state: bfloat16 [3, 1024, 8192], P(None, ('groups', 'dp'), 'tensor'), parts along dimension 1, may hold values from -6 to 6
- x_weight: bfloat16 [8192, 544], P('tensor'), may hold values from -0.0625 to 0.0625
- dt_weight: bfloat16 [512, 8192], P(None, 'tensor'), may hold values from -0.25 to 0.25
- dt_bias: float32 [8192], P('tensor'), may hold values from -6.9 to -2.3
- a_log: float32 [16, 8192], P(None, 'tensor'), may hold values from 0 to 2.77
- d_skip: float32 [8192], P('tensor'), may hold values from 0.5 to 1.5
- ssm_state: bfloat16 [1024, 16, 8192], P(('groups', 'dp'), None, 'tensor'), parts along dimension 0, may hold values from -6 to 6
- out_weight: bfloat16 [8192, 8192], P('tensor', 'dp'), may hold values from -0.09375 to 0.09375
- mamba_gain: float32 [8192], replicated, may hold values from 0.5 to 1.5
- moe_gain: float32 [8192], replicated, may hold values from 0.5 to 2
- up_weight: bfloat16 [8192, 24576], P(None, ('tensor', 'dp')), may hold values from -0.0625 to 0.0625
- down_weight: bfloat16 [24576, 8192], P(('tensor', 'dp')), may hold values from -0.078125 to 0.078125
- expert_ids: int32 [1024, 2], P(('groups', 'dp')), parts along dimension 0, may hold values from 0 to 15, as said below
- slot_index: int32 [1024, 2], P(('groups', 'dp')), parts along dimension 0, may hold values from 0 to 64, as said below
- counts: int32 [32], P('groups'), parts along dimension 0, may hold values from 0 to 64, as said below
- route_weight: float32 [1024, 2], P(('groups', 'dp')), parts along dimension 0, may hold values from 0.2 to 1
Outputs:
- mixed: bfloat16 [1024, 8192], P(('groups', 'dp'), 'tensor'), parts along dimension 0
The draws below stay inside these ranges and needn't reach their ends.
There are 2 independent parts, one for each index of `groups`. The reference program is written for one: setup_inputs(seed, part) draws one part's arguments, and reference() takes and returns one part's arrays. A program takes and returns all parts, laid end to end along the dimension named above; an argument that names none is the same for every part. Nothing has to cross between parts.
Inputs may be any that keep to these rules, and one draw needn't show every extreme that they name: `expert_ids`: the two experts of a request differ. Some expert below 2 is named by 64 rows or more. `slot_index`: rows naming one expert are numbered 0, 1, 2 in order of request and then of k; numbers of 64 or more are given as 64. counts[e] is at most the number of rows naming e with slot under 64; for some expert below 2 it is 64.
All inputs are finite; a program needn't handle non-finite values.
Results may differ from the reference program's by a relative error of at most 0.019.
Values may be sent and summed in bfloat16 or wider, within the bound.
A program may use at most 384 MiB of HBM per device.

```python
import math
import jax
import jax.numpy as jnp
from jax import lax

D = 8192
E_WIN = 8192
NSTATE = 16
RANK = 512
EXPERTS = 16
TOP = 2
EXP_WIN = 2
FF_WIN = 12288
REQUESTS = 512
CAP = 64
N_TENSOR = 4


def routing(key):
    keys = jax.random.split(key, 5)
    first = jax.random.randint(keys[0], (REQUESTS,), 0, EXPERTS)
    offset = jax.random.randint(keys[1], (REQUESTS,), 1, EXPERTS)
    chosen = jax.random.randint(keys[2], (), 0, EXP_WIN)
    order = jax.random.permutation(keys[3], REQUESTS)
    forced = jnp.zeros((REQUESTS,), jnp.int32).at[order[:CAP]].set(1)
    first = jnp.where(forced == 1, chosen, first)
    second = (first + offset) % EXPERTS
    expert_table = jnp.stack([first, second], 1).astype(jnp.int32)
    flat_ids = expert_table.reshape(-1)
    onehot = (flat_ids[:, None] == jnp.arange(EXPERTS, dtype=jnp.int32)[None, :]).astype(jnp.int32)
    before = jnp.cumsum(onehot, 0) - onehot
    ranks = jnp.sum(before * onehot, 1)
    slot_table = jnp.minimum(ranks, CAP).reshape(REQUESTS, TOP).astype(jnp.int32)
    bounds = jax.random.randint(keys[4], (EXPERTS,), CAP // 2, CAP + 1)
    count_table = jnp.minimum(jnp.minimum(jnp.sum(onehot, 0), CAP), bounds)
    count_table = count_table.at[chosen].set(CAP).astype(jnp.int32)
    return (expert_table, slot_table, count_table)


def draw_expert_ids(key, part):
    return routing(key)[0]


def draw_slot_index(key, part):
    return routing(key)[1]


def draw_counts(key, part):
    return routing(key)[2]


def raised(values, own_key, source, target, shards_of, factor):
    def block_of(position):
        return (jnp.arange(values.shape[position]) // (values.shape[position] // shards_of)).reshape((-1,) + (1,) * (values.ndim - 1 - position))

    one_side = jax.random.permutation(own_key, shards_of)[block_of(target)]
    far = (block_of(target) + shards_of // 2) % shards_of
    return jnp.where((block_of(source) == one_side) | (block_of(source) == far), factor * values, values)


def steps_of(stream_key, extent, cuts, smallest, top_value):
    def one(dim, parts):
        draws = jax.random.uniform(jax.random.fold_in(jax.random.fold_in(stream_key, 6), dim), (parts,), jnp.float32, smallest / len(cuts), top_value / len(cuts))
        return jnp.repeat(jnp.exp(draws), extent[dim] // parts).reshape((-1,) + (1,) * (len(extent) - dim - 1))

    factor_of = one(*cuts[0])
    for cut in cuts[1:]:
        factor_of = factor_of * one(*cut)
    return factor_of


def gaussian(key, dims, width, most, shards=(), kind=jnp.bfloat16):
    level = steps_of(key, dims, shards, -0.22, 0.18) if shards else 1.0
    values = jax.random.normal(key, dims, jnp.float32) * width * level
    return jnp.minimum(jnp.maximum(values, -most), most).astype(kind)


def noise_with(rng, dims, deviation, most, cuts, heavy, kind=jnp.bfloat16):
    entries = deviation * jax.random.normal(rng, dims, jnp.float32)
    if cuts:
        entries = entries * steps_of(rng, dims, cuts, -0.22, 0.18)
    return jnp.clip(raised(entries, jax.random.fold_in(rng, 3), *heavy), -most, most).astype(kind)


def setup_inputs(seed: int = 0, part: int = 0) -> dict:
    arg_keys = jax.random.split(jax.random.key(seed), 21)
    own_keys = jax.random.split(jax.random.fold_in(arg_keys[20], part), 21)
    return {
        "tokens": gaussian(own_keys[0], (REQUESTS, D), 1.0, 6.0, ((0, 4), (1, 4))),
        "in_weight": gaussian(arg_keys[1], (D, 2, E_WIN), D ** -0.5, 0.0625, ((0, 4), (2, 4))),
        "conv_weight": gaussian(arg_keys[2], (4, E_WIN), 4 ** -0.5, 3.0, ((1, 4),), jnp.float32),
        "conv_bias": gaussian(arg_keys[3], (E_WIN,), 0.5, 3.0, ((0, 4),), jnp.float32),
        "conv_state": gaussian(own_keys[4], (3, REQUESTS, E_WIN), 1.0, 6.0, ((1, 4), (2, 4))),
        "x_weight": gaussian(arg_keys[5], (E_WIN, RANK + 2 * NSTATE), E_WIN ** -0.5, 0.0625, ((0, 4),)),
        "dt_weight": gaussian(arg_keys[6], (RANK, E_WIN), RANK ** -0.5, 0.25, ((1, 4),)),
        "dt_bias": jnp.clip(-6.9 + 4.6000001430511475 * jax.random.uniform(arg_keys[7], (E_WIN,), jnp.float32) ** steps_of(arg_keys[7], (E_WIN,), ((0, 4),), -0.2, 0.2), -6.9, -2.3),
        "a_log": jnp.clip(2.77 * jax.random.uniform(arg_keys[8], (NSTATE, E_WIN), jnp.float32) ** steps_of(arg_keys[8], (NSTATE, E_WIN), ((1, 4),), -0.2, 0.2), 0.0, 2.77),
        "d_skip": jnp.clip(1.0 + 0.1 * jax.random.normal(arg_keys[9], (E_WIN,), jnp.float32), 0.5, 1.5),
        "ssm_state": gaussian(own_keys[10], (REQUESTS, NSTATE, E_WIN), 1.0, 6.0, ((0, 4), (2, 4))),
        "out_weight": noise_with(arg_keys[11], (E_WIN, D), E_WIN ** -0.5, 0.09375, ((0, 4), (1, 4)), (0, 1, 4, 2.0)),
        "mamba_gain": jnp.clip(1.0 + 0.1 * jax.random.normal(arg_keys[12], (D,), jnp.float32), 0.5, 1.5),
        "moe_gain": jnp.clip(jnp.exp(jax.random.uniform(arg_keys[13], (D,), jnp.float32, math.log(0.5), math.log(2.0))), 0.5, 2.0),
        "up_weight": gaussian(arg_keys[14], (D, EXP_WIN * FF_WIN), D ** -0.5, 0.0625, ((1, 16),)),
        "down_weight": noise_with(arg_keys[15], (EXP_WIN * FF_WIN, D), FF_WIN ** -0.5, 0.078125, ((0, 16),), (0, 1, 16, 2.0)),
        "expert_ids": draw_expert_ids(jax.random.fold_in(jax.random.fold_in(arg_keys[20], part), 71), part),
        "slot_index": draw_slot_index(jax.random.fold_in(jax.random.fold_in(arg_keys[20], part), 71), part),
        "counts": draw_counts(jax.random.fold_in(jax.random.fold_in(arg_keys[20], part), 71), part),
        "route_weight": jnp.clip(0.2 + 0.8 * jax.random.uniform(own_keys[19], (REQUESTS, TOP), jnp.float32) ** steps_of(own_keys[19], (REQUESTS, TOP), ((0, 4),), -0.2, 0.2), 0.2, 1.0),
    }


EPS = 1e-05

def reference(tokens, in_weight, conv_weight, conv_bias, conv_state, x_weight, dt_weight, dt_bias, a_log, d_skip, ssm_state, out_weight, mamba_gain, moe_gain, up_weight, down_weight, expert_ids, slot_index, counts, route_weight):
    stream = tokens.astype(jnp.float32)
    normed = (stream * lax.rsqrt(lax.optimization_barrier(jnp.mean(stream * stream, -1, keepdims=True)) + EPS) * mamba_gain).astype(jnp.bfloat16)
    projected = jnp.dot(normed, in_weight.reshape(D, 2 * E_WIN), preferred_element_type=jnp.float32).reshape(REQUESTS, 2, E_WIN)
    inner_part = projected[:, 0]
    gate_part = projected[:, 1]
    history = conv_state.astype(jnp.float32)
    conv_out = conv_bias + conv_weight[3] * inner_part + conv_weight[0] * history[0] + conv_weight[1] * history[1] + conv_weight[2] * history[2]
    activated = jax.nn.silu(conv_out)
    ssm_inputs = jnp.dot(activated.astype(jnp.bfloat16), x_weight, preferred_element_type=jnp.float32)
    step_low = ssm_inputs[:, :RANK].astype(jnp.bfloat16)
    input_map = ssm_inputs[:, RANK:RANK + NSTATE]
    output_map = ssm_inputs[:, RANK + NSTATE:]
    step_size = jax.nn.softplus(jnp.dot(step_low, dt_weight, preferred_element_type=jnp.float32) + dt_bias)
    rates = -jnp.exp(a_log)
    readout = d_skip * activated
    for index in range(NSTATE):
        state_row = jnp.exp(step_size * rates[index]) * ssm_state[:, index].astype(jnp.float32) + step_size * input_map[:, index:index + 1] * activated
        readout = readout + output_map[:, index:index + 1] * state_row
    gated = (readout * jax.nn.silu(gate_part)).astype(jnp.bfloat16)
    span = E_WIN // N_TENSOR

    def add_shard(shard, total):
        start = (shard * span).astype(jnp.int32)
        piece = jnp.dot(lax.dynamic_slice_in_dim(gated, start, span, 1), lax.dynamic_slice_in_dim(out_weight, start, span, 0), preferred_element_type=jnp.float32)
        rounded = lax.optimization_barrier(piece.astype(jnp.bfloat16))
        return total + rounded.astype(jnp.float32)
    mamba_sum = lax.fori_loop(jnp.int32(0), jnp.int32(N_TENSOR), add_shard, jnp.zeros((REQUESTS, D), jnp.float32))
    residual = (stream + mamba_sum).astype(jnp.bfloat16)
    carried = residual.astype(jnp.float32)
    moe_rows = (carried * moe_gain).astype(jnp.bfloat16)
    limit = counts[expert_ids]
    valid = (expert_ids < EXP_WIN) & (slot_index < limit)
    target = jnp.where(valid, expert_ids * CAP + slot_index, EXP_WIN * CAP).astype(jnp.int32)
    buffer = jnp.zeros((EXP_WIN * CAP + 1, D), jnp.bfloat16).at[target.reshape(-1)].set(jnp.repeat(moe_rows, TOP, axis=0))
    results = []
    for expert in range(EXP_WIN):
        rows = buffer[expert * CAP:(expert + 1) * CAP]
        hidden = jax.nn.silu(jnp.dot(rows, up_weight[:, expert * FF_WIN:(expert + 1) * FF_WIN], preferred_element_type=jnp.float32)).astype(jnp.bfloat16)
        results.append(jnp.dot(hidden, down_weight[expert * FF_WIN:(expert + 1) * FF_WIN], preferred_element_type=jnp.float32))
    results.append(jnp.zeros((1, D), jnp.float32))
    expert_out = jnp.concatenate(results, 0)
    weights = jnp.where(valid, route_weight, jnp.float32(0.0))
    moe_sum = weights[:, 0:1] * expert_out[target[:, 0]] + weights[:, 1:2] * expert_out[target[:, 1]]
    return (carried + moe_sum).astype(jnp.bfloat16)
```

```python
import jax
import jax.numpy as jnp
from jax import lax
from jax.sharding import PartitionSpec as P

NSTATE = 16
RANK = 512
EXPERTS = 16
TOP = 2
EXP_WIN = 2


EPS = 1e-05


def shards(
    tokens,
    in_weight,
    conv_weight,
    conv_bias,
    conv_state,
    x_weight,
    dt_weight,
    dt_bias,
    a_log,
    d_skip,
    ssm_state,
    out_weight,
    mamba_gain,
    moe_gain,
    up_weight,
    down_weight,
    expert_ids,
    slot_index,
    counts,
    route_weight,
):
    req_rows = tokens.shape[0]
    chans = in_weight.shape[2]
    own32 = tokens.astype(jnp.float32)
    feats = tokens.shape[1]
    gain_own = lax.dynamic_slice_in_dim(
        mamba_gain, lax.axis_index("tensor") * feats, feats, 0
    )
    scaled = (own32 * gain_own).astype(jnp.bfloat16)
    square_sum = lax.psum(jnp.sum(own32 * own32, -1, keepdims=True), "tensor")
    inverse = lax.rsqrt(square_sum / mamba_gain.shape[0] + EPS)
    whole = lax.all_gather(scaled, "tensor", axis=1, tiled=True)
    part_rows = lax.all_to_all(whole, "dp", split_axis=1, concat_axis=0, tiled=True)
    weight = in_weight.reshape(in_weight.shape[0], 2 * chans)
    terms = jnp.dot(part_rows, weight, preferred_element_type=jnp.float32)
    projected = lax.psum_scatter(
        terms.astype(jnp.bfloat16), "dp", scatter_dimension=0, tiled=True
    ).astype(jnp.float32)
    projected = (projected * inverse).reshape(req_rows, 2, chans)
    inner_part = projected[:, 0]
    gate_part = projected[:, 1]
    history = conv_state.astype(jnp.float32)
    conv_out = (
        conv_bias
        + conv_weight[3] * inner_part
        + conv_weight[0] * history[0]
        + conv_weight[1] * history[1]
        + conv_weight[2] * history[2]
    )
    activated = jax.nn.silu(conv_out)
    local_inputs = jnp.dot(
        activated.astype(jnp.bfloat16), x_weight, preferred_element_type=jnp.float32
    )
    ssm_inputs = lax.psum(local_inputs.astype(jnp.bfloat16), "tensor").astype(jnp.float32)
    step_low = ssm_inputs[:, :RANK].astype(jnp.bfloat16)
    input_map = ssm_inputs[:, RANK : RANK + NSTATE]
    output_map = ssm_inputs[:, RANK + NSTATE :]
    step_size = jax.nn.softplus(
        jnp.dot(step_low, dt_weight, preferred_element_type=jnp.float32) + dt_bias
    )
    rates = -jnp.exp(a_log)
    readout = d_skip * activated
    for index in range(NSTATE):
        state_row = (
            jnp.exp(step_size * rates[index]) * ssm_state[:, index].astype(jnp.float32)
            + step_size * input_map[:, index : index + 1] * activated
        )
        readout = readout + output_map[:, index : index + 1] * state_row
    gated = (readout * jax.nn.silu(gate_part)).astype(jnp.bfloat16)
    gated_all = lax.all_gather(gated, "dp", axis=0, tiled=True)
    out_cols = jnp.dot(gated_all, out_weight, preferred_element_type=jnp.float32)
    out_terms = lax.all_to_all(
        out_cols.astype(jnp.bfloat16), "dp", split_axis=0, concat_axis=1, tiled=True
    )
    mamba_sum = lax.psum_scatter(
        out_terms, "tensor", scatter_dimension=1, tiled=True
    ).astype(jnp.float32)
    residual = (tokens.astype(jnp.float32) + mamba_sum).astype(jnp.bfloat16)
    carried = residual.astype(jnp.float32)
    feat_cols = carried.shape[1]
    gain_slice = lax.dynamic_slice_in_dim(
        moe_gain, lax.axis_index("tensor") * feat_cols, feat_cols, 0
    )
    moe_rows = (carried * gain_slice).astype(jnp.bfloat16)
    capacity = req_rows * lax.axis_size("dp") * TOP // EXPERTS
    limit = jnp.sum(
        (expert_ids[:, :, None] == jnp.arange(EXPERTS, dtype=jnp.int32)[None, None, :])
        * counts[None, None, :],
        -1,
    )
    valid = (expert_ids < EXP_WIN) & (slot_index < limit)
    target = jnp.where(valid, expert_ids * capacity + slot_index, EXP_WIN * capacity)
    positions = jnp.arange(EXP_WIN * capacity, dtype=jnp.int32)
    slot_match = (positions[:, None] == target[None, :, 0]) | (
        positions[:, None] == target[None, :, 1]
    )
    local_buffer = jnp.dot(
        slot_match.astype(jnp.bfloat16), moe_rows, preferred_element_type=jnp.float32
    ).reshape(EXP_WIN, capacity, feat_cols)
    buffer = lax.psum(local_buffer.astype(jnp.bfloat16), "dp")
    per_expert = lax.axis_size("tensor") // EXP_WIN
    own_expert = lax.axis_index("tensor") // per_expert
    rows = lax.dynamic_index_in_dim(
        lax.all_gather(buffer, "tensor", axis=2, tiled=True), own_expert, 0, keepdims=False
    )
    pre_act = jnp.dot(rows, up_weight, preferred_element_type=jnp.float32)
    hidden = jax.nn.silu(pre_act).astype(jnp.bfloat16)
    partial_out = jnp.dot(hidden, down_weight, preferred_element_type=jnp.float32)
    expert_mask = (jnp.arange(EXP_WIN, dtype=jnp.int32) == own_expert)[:, None, None]
    spread_term = jnp.where(expert_mask, partial_out[None], jnp.float32(0.0))
    feature_sums = lax.psum_scatter(
        spread_term.astype(jnp.bfloat16), "tensor", scatter_dimension=2, tiled=True
    )
    expert_out = lax.psum(feature_sums, "dp").astype(jnp.float32)
    weights = jnp.where(valid, route_weight, jnp.float32(0.0))
    selector = jnp.where(
        positions[None, :] == target[:, 0:1], weights[:, 0:1], jnp.float32(0.0)
    ) + jnp.where(positions[None, :] == target[:, 1:2], weights[:, 1:2], jnp.float32(0.0))
    moe_sum = jnp.dot(
        selector,
        expert_out.reshape(EXP_WIN * capacity, feat_cols),
        precision=lax.Precision.HIGHEST,
        preferred_element_type=jnp.float32,
    )
    return (carried + moe_sum).astype(jnp.bfloat16)


def solution(mesh):
    placed = (
        P(("groups", "dp"), "tensor"),
        P("dp", None, "tensor"),
        P(None, "tensor"),
        P("tensor"),
        P(None, ("groups", "dp"), "tensor"),
        P("tensor", None),
        P(None, "tensor"),
        P("tensor"),
        P(None, "tensor"),
        P("tensor"),
        P(("groups", "dp"), None, "tensor"),
        P("tensor", "dp"),
        P(),
        P(),
        P(None, ("tensor", "dp")),
        P(("tensor", "dp"), None),
        P(("groups", "dp"), None),
        P(("groups", "dp"), None),
        P("groups"),
        P(("groups", "dp"), None),
    )
    return jax.shard_map(
        shards, mesh=mesh, in_specs=placed, out_specs=P(("groups", "dp"), "tensor"), check_vma=False
    )
```

```python
import jax
import jax.numpy as jnp
from jax import lax
from jax.experimental import pallas as pl
from jax.experimental.pallas import tpu as pltpu
from jax.sharding import PartitionSpec as P

NSTATE = 16
RANK = 512
EXPERTS = 16
TOP = 2
EXP_WIN = 2


EPS = 1e-05


def exchange(x, axis, call_id, out_shape, source, place):
    n = lax.axis_size(axis)

    def kernel(x_ref, out_ref, own_sem, send_sem, recv_sem):
        me = lax.axis_index(axis)
        barrier = pltpu.get_barrier_semaphore()
        for k in range(1, n):
            pl.semaphore_signal(
                barrier,
                inc=1,
                device_id={axis: lax.rem(me + k, n)},
                device_id_type=pl.DeviceIdType.MESH,
            )
        pl.semaphore_wait(barrier, n - 1)
        copies = []
        for k in range(1, n):
            peer = lax.rem(me + k, n)
            copies.append(
                pltpu.make_async_remote_copy(
                    src_ref=x_ref.at[source(peer)],
                    dst_ref=out_ref.at[place(me)],
                    send_sem=send_sem.at[k],
                    recv_sem=recv_sem.at[k],
                    device_id={axis: peer},
                    device_id_type=pl.DeviceIdType.MESH,
                )
            )
        for copy in copies:
            copy.start()
        own = pltpu.make_async_copy(x_ref.at[source(me)], out_ref.at[place(me)], own_sem)
        own.start()
        own.wait()
        for copy in copies:
            copy.wait()

    return pl.pallas_call(
        kernel,
        out_shape=jax.ShapeDtypeStruct(out_shape, x.dtype),
        in_specs=[pl.BlockSpec(memory_space=pl.ANY)],
        out_specs=pl.BlockSpec(memory_space=pl.ANY),
        scratch_shapes=[
            pltpu.SemaphoreType.DMA,
            pltpu.SemaphoreType.DMA((n,)),
            pltpu.SemaphoreType.DMA((n,)),
        ],
        compiler_params=pltpu.CompilerParams(collective_id=call_id, has_side_effects=True),
        name="exchange_%d" % call_id,
    )(x)


def rows_at(size):
    return lambda i: (pl.ds(pl.multiple_of(i * size, size), size), slice(None))


def cols_at(size):
    return lambda i: (slice(None), pl.ds(pl.multiple_of(i * size, size), size))


def block_at(i):
    return (i,)


def whole_at(i):
    return (slice(None),)


def shards(
    tokens,
    in_weight,
    conv_weight,
    conv_bias,
    conv_state,
    x_weight,
    dt_weight,
    dt_bias,
    a_log,
    d_skip,
    ssm_state,
    out_weight,
    mamba_gain,
    moe_gain,
    up_weight,
    down_weight,
    expert_ids,
    slot_index,
    counts,
    route_weight,
):
    req_rows = tokens.shape[0]
    chans = in_weight.shape[2]
    dp = lax.axis_size("dp")
    n_tensor = lax.axis_size("tensor")
    whole = lax.all_gather(tokens, "tensor", axis=1, tiled=True)
    whole32 = whole.astype(jnp.float32)
    normed = (
        whole32 * lax.rsqrt(jnp.mean(whole32 * whole32, -1, keepdims=True) + EPS) * mamba_gain
    ).astype(jnp.bfloat16)
    in_rows = in_weight.shape[0]
    part_rows = exchange(
        normed, "dp", 0, (dp * req_rows, in_rows), cols_at(in_rows), rows_at(req_rows)
    )
    weight = in_weight.reshape(in_weight.shape[0], 2 * chans)
    terms = jnp.dot(part_rows, weight, preferred_element_type=jnp.float32)
    projected = lax.psum_scatter(
        terms.astype(jnp.bfloat16), "dp", scatter_dimension=0, tiled=True
    ).astype(jnp.float32)
    projected = projected.reshape(req_rows, 2, chans)
    inner_part = projected[:, 0]
    gate_part = projected[:, 1]
    history = conv_state.astype(jnp.float32)
    conv_out = (
        conv_bias
        + conv_weight[3] * inner_part
        + conv_weight[0] * history[0]
        + conv_weight[1] * history[1]
        + conv_weight[2] * history[2]
    )
    activated = jax.nn.silu(conv_out)
    local_inputs = jnp.dot(
        activated.astype(jnp.bfloat16), x_weight, preferred_element_type=jnp.float32
    )
    low = local_inputs.astype(jnp.bfloat16)
    ssm_inputs = jnp.sum(
        exchange(low, "tensor", 1, (n_tensor,) + low.shape, whole_at, block_at).astype(
            jnp.float32
        ),
        0,
    )
    step_low = ssm_inputs[:, :RANK].astype(jnp.bfloat16)
    input_map = ssm_inputs[:, RANK : RANK + NSTATE]
    output_map = ssm_inputs[:, RANK + NSTATE :]
    step_size = jax.nn.softplus(
        jnp.dot(step_low, dt_weight, preferred_element_type=jnp.float32) + dt_bias
    )
    rates = -jnp.exp(a_log)
    readout = d_skip * activated
    for index in range(NSTATE):
        state_row = (
            jnp.exp(step_size * rates[index]) * ssm_state[:, index].astype(jnp.float32)
            + step_size * input_map[:, index : index + 1] * activated
        )
        readout = readout + output_map[:, index : index + 1] * state_row
    gated = (readout * jax.nn.silu(gate_part)).astype(jnp.bfloat16)
    gated_all = lax.all_gather(gated, "dp", axis=0, tiled=True)
    out_cols = jnp.dot(gated_all, out_weight, preferred_element_type=jnp.float32)
    out_chunk = out_weight.shape[1]
    out_terms = exchange(
        out_cols.astype(jnp.bfloat16),
        "dp",
        2,
        (req_rows, dp * out_chunk),
        rows_at(req_rows),
        cols_at(out_chunk),
    )
    mamba_sum = lax.psum_scatter(
        out_terms, "tensor", scatter_dimension=1, tiled=True
    ).astype(jnp.float32)
    residual = (tokens.astype(jnp.float32) + mamba_sum).astype(jnp.bfloat16)
    carried = residual.astype(jnp.float32)
    feat_cols = carried.shape[1]
    gain_slice = lax.dynamic_slice_in_dim(
        moe_gain, lax.axis_index("tensor") * feat_cols, feat_cols, 0
    )
    moe_rows = (carried * gain_slice).astype(jnp.bfloat16)
    capacity = req_rows * lax.axis_size("dp") * TOP // EXPERTS
    limit = jnp.sum(
        (expert_ids[:, :, None] == jnp.arange(EXPERTS, dtype=jnp.int32)[None, None, :])
        * counts[None, None, :],
        -1,
    )
    valid = (expert_ids < EXP_WIN) & (slot_index < limit)
    target = jnp.where(valid, expert_ids * capacity + slot_index, EXP_WIN * capacity)
    part_slots = capacity // dp
    positions = (
        jnp.arange(EXP_WIN * capacity, dtype=jnp.int32)
        .reshape(EXP_WIN, dp, part_slots)
        .transpose(1, 0, 2)
        .reshape(-1)
    )
    slot_match = (positions[:, None] == target[None, :, 0]) | (
        positions[:, None] == target[None, :, 1]
    )
    local_buffer = jnp.dot(
        slot_match.astype(jnp.bfloat16), moe_rows, preferred_element_type=jnp.float32
    ).astype(jnp.bfloat16)
    part_shape = (dp, EXP_WIN * part_slots, feat_cols)
    filled = exchange(
        local_buffer, "dp", 3, part_shape, rows_at(EXP_WIN * part_slots), block_at
    )
    filled = jnp.sum(filled.astype(jnp.float32), 0).astype(jnp.bfloat16)
    per_expert = n_tensor // EXP_WIN
    features = n_tensor * feat_cols
    own_rows = exchange(
        filled,
        "tensor",
        4,
        (part_slots, features),
        lambda i: rows_at(part_slots)(lax.div(i, per_expert)),
        cols_at(feat_cols),
    )
    rows = exchange(own_rows, "dp", 5, (capacity, features), whole_at, rows_at(part_slots))
    pre_act = jnp.dot(rows, up_weight, preferred_element_type=jnp.float32)
    hidden = jax.nn.silu(pre_act).astype(jnp.bfloat16)
    partial_out = jnp.dot(hidden, down_weight, preferred_element_type=jnp.float32)
    shares = exchange(
        partial_out.astype(jnp.bfloat16),
        "dp",
        6,
        (dp, part_slots, features),
        rows_at(part_slots),
        block_at,
    )
    shares = jnp.sum(shares.astype(jnp.float32), 0).astype(jnp.bfloat16)
    shares = exchange(
        shares, "tensor", 7, (n_tensor, part_slots, feat_cols), cols_at(feat_cols), block_at
    )
    shares = jnp.sum(
        shares.astype(jnp.float32).reshape(EXP_WIN, per_expert, part_slots, feat_cols), 1
    ).astype(jnp.bfloat16)
    expert_out = exchange(
        shares.reshape(EXP_WIN * part_slots, feat_cols),
        "dp",
        8,
        part_shape,
        whole_at,
        block_at,
    ).astype(jnp.float32)
    weights = jnp.where(valid, route_weight, jnp.float32(0.0))
    selector = jnp.where(
        positions[None, :] == target[:, 0:1], weights[:, 0:1], jnp.float32(0.0)
    ) + jnp.where(positions[None, :] == target[:, 1:2], weights[:, 1:2], jnp.float32(0.0))
    moe_sum = jnp.dot(
        selector,
        expert_out.reshape(EXP_WIN * capacity, feat_cols),
        precision=lax.Precision.HIGHEST,
        preferred_element_type=jnp.float32,
    )
    return (carried + moe_sum).astype(jnp.bfloat16)


def solution(mesh):
    placed = (
        P(("groups", "dp"), "tensor"),
        P("dp", None, "tensor"),
        P(None, "tensor"),
        P("tensor"),
        P(None, ("groups", "dp"), "tensor"),
        P("tensor", None),
        P(None, "tensor"),
        P("tensor"),
        P(None, "tensor"),
        P("tensor"),
        P(("groups", "dp"), None, "tensor"),
        P("tensor", "dp"),
        P(),
        P(),
        P(None, ("tensor", "dp")),
        P(("tensor", "dp"), None),
        P(("groups", "dp"), None),
        P(("groups", "dp"), None),
        P("groups"),
        P(("groups", "dp"), None),
    )
    return jax.shard_map(
        shards, mesh=mesh, in_specs=placed, out_specs=P(("groups", "dp"), "tensor"), check_vma=False
    )
```

```python
import jax
import jax.numpy as jnp
from jax import lax
from jax.experimental import pallas as pl
from jax.experimental.pallas import tpu as pltpu
from jax.sharding import PartitionSpec as P

NSTATE = 16
RANK = 512
EXPERTS = 16
TOP = 2
EXP_WIN = 2


EPS = 1e-05


def exchange(x, axis, call_id, out_shape, source, place):
    n = lax.axis_size(axis)

    def kernel(x_ref, out_ref, own_sem, send_sem, recv_sem):
        me = lax.axis_index(axis)
        barrier = pltpu.get_barrier_semaphore()
        for k in range(1, n):
            pl.semaphore_signal(
                barrier,
                inc=1,
                device_id={axis: lax.rem(me + k, n)},
                device_id_type=pl.DeviceIdType.MESH,
            )
        pl.semaphore_wait(barrier, n - 1)
        copies = []
        for k in range(1, n):
            peer = lax.rem(me + k, n)
            copies.append(
                pltpu.make_async_remote_copy(
                    src_ref=x_ref.at[source(peer)],
                    dst_ref=out_ref.at[place(me)],
                    send_sem=send_sem.at[k],
                    recv_sem=recv_sem.at[k],
                    device_id={axis: peer},
                    device_id_type=pl.DeviceIdType.MESH,
                )
            )
        for copy in copies:
            copy.start()
        own = pltpu.make_async_copy(x_ref.at[source(me)], out_ref.at[place(me)], own_sem)
        own.start()
        own.wait()
        for copy in copies:
            copy.wait()

    return pl.pallas_call(
        kernel,
        out_shape=jax.ShapeDtypeStruct(out_shape, x.dtype),
        in_specs=[pl.BlockSpec(memory_space=pl.ANY)],
        out_specs=pl.BlockSpec(memory_space=pl.ANY),
        scratch_shapes=[
            pltpu.SemaphoreType.DMA,
            pltpu.SemaphoreType.DMA((n,)),
            pltpu.SemaphoreType.DMA((n,)),
        ],
        compiler_params=pltpu.CompilerParams(collective_id=call_id, has_side_effects=True),
        name="exchange_%d" % call_id,
    )(x)


def rows_at(size):
    return lambda i: (pl.ds(pl.multiple_of(i * size, size), size), slice(None))


def cols_at(size):
    return lambda i: (slice(None), pl.ds(pl.multiple_of(i * size, size), size))


def block_at(i):
    return (i,)


def whole_at(i):
    return (slice(None),)


def gather_pairs(x, axis, call_id):
    n = lax.axis_size(axis)
    rows = x.shape[0]
    if n != 4:
        return exchange(x, axis, call_id, (n * rows,) + x.shape[1:], whole_at, rows_at(rows))

    def kernel(x_ref, out_ref, own_sem, send_sem, recv_sem):
        me = lax.axis_index(axis)
        far = lax.rem(me + 2, 4)
        sibling = me + 1 - 2 * lax.rem(me, 2)
        barrier = pltpu.get_barrier_semaphore()
        for peer in (far, sibling):
            pl.semaphore_signal(
                barrier, inc=1, device_id={axis: peer}, device_id_type=pl.DeviceIdType.MESH
            )
        pl.semaphore_wait(barrier, 2)
        place = rows_at(rows)

        def send(source, owner, peer, k):
            return pltpu.make_async_remote_copy(
                src_ref=source,
                dst_ref=out_ref.at[place(owner)],
                send_sem=send_sem.at[k],
                recv_sem=recv_sem.at[k],
                device_id={axis: peer},
                device_id_type=pl.DeviceIdType.MESH,
            )

        across = send(x_ref, me, far, 0)
        beside = send(x_ref, me, sibling, 1)
        across.start()
        beside.start()
        own = pltpu.make_async_copy(x_ref, out_ref.at[place(me)], own_sem)
        own.start()
        own.wait()
        across.wait_recv()
        onward = send(out_ref.at[place(far)], far, sibling, 2)
        onward.start()
        across.wait_send()
        beside.wait()
        onward.wait()

    return pl.pallas_call(
        kernel,
        out_shape=jax.ShapeDtypeStruct((n * rows,) + x.shape[1:], x.dtype),
        in_specs=[pl.BlockSpec(memory_space=pl.ANY)],
        out_specs=pl.BlockSpec(memory_space=pl.ANY),
        scratch_shapes=[
            pltpu.SemaphoreType.DMA,
            pltpu.SemaphoreType.DMA((3,)),
            pltpu.SemaphoreType.DMA((3,)),
        ],
        compiler_params=pltpu.CompilerParams(collective_id=call_id, has_side_effects=True),
        name="gather_%d" % call_id,
    )(x)


def scan_kernel(
    state_ref, step_ref, act_ref, gate_ref, in_ref, out_map_ref, rates_ref, skip_ref, o_ref, acc_ref
):
    rows, chans = act_ref.shape
    width = min(512, chans)
    for start in range(0, chans, width):
        cols = slice(start, start + width)
        rates = rates_ref[:, cols]
        for r in range(rows):
            step = step_ref[r : r + 1, cols]
            driven = step * act_ref[r : r + 1, cols]
            new = jnp.exp(step * rates) * state_ref[r, :, cols].astype(jnp.float32)
            new = new + driven * in_ref[r]
            acc_ref[r : r + 1, cols] = jnp.sum(out_map_ref[r] * new, 0, keepdims=True)
    gate = gate_ref[...]
    readout = skip_ref[...] * act_ref[...] + acc_ref[...]
    o_ref[...] = (readout * (gate / (1.0 + jnp.exp(-gate)))).astype(o_ref.dtype)


def scan(state, step_size, activated, gate, input_map, output_map, rates, d_skip):
    total, chans = activated.shape
    rows = 16
    flat = pl.BlockSpec((rows, chans), lambda i: (i, 0))
    column = pl.BlockSpec((rows, NSTATE, 1), lambda i: (i, 0, 0))
    return pl.pallas_call(
        scan_kernel,
        grid=(total // rows,),
        out_shape=jax.ShapeDtypeStruct((total, chans), jnp.bfloat16),
        in_specs=[
            pl.BlockSpec((rows, NSTATE, chans), lambda i: (i, 0, 0)),
            flat,
            flat,
            flat,
            column,
            column,
            pl.BlockSpec((NSTATE, chans), lambda i: (0, 0)),
            pl.BlockSpec((1, chans), lambda i: (0, 0)),
        ],
        out_specs=flat,
        scratch_shapes=[pltpu.VMEM((rows, chans), jnp.float32)],
        compiler_params=pltpu.CompilerParams(vmem_limit_bytes=32 * 2**20),
        cost_estimate=pl.CostEstimate(
            flops=8 * total * NSTATE * chans,
            bytes_accessed=2 * total * NSTATE * chans,
            transcendentals=total * NSTATE * chans,
        ),
        name="scan",
    )(
        state,
        step_size,
        activated,
        gate,
        input_map[:, :, None],
        output_map[:, :, None],
        rates,
        d_skip[None, :],
    )


def shards(
    tokens,
    in_weight,
    conv_weight,
    conv_bias,
    conv_state,
    x_weight,
    dt_weight,
    dt_bias,
    a_log,
    d_skip,
    ssm_state,
    out_weight,
    mamba_gain,
    moe_gain,
    up_weight,
    down_weight,
    expert_ids,
    slot_index,
    counts,
    route_weight,
):
    req_rows = tokens.shape[0]
    chans = in_weight.shape[2]
    dp = lax.axis_size("dp")
    n_tensor = lax.axis_size("tensor")
    whole = lax.all_gather(tokens, "tensor", axis=1, tiled=True)
    whole32 = whole.astype(jnp.float32)
    normed = (
        whole32 * lax.rsqrt(jnp.mean(whole32 * whole32, -1, keepdims=True) + EPS) * mamba_gain
    ).astype(jnp.bfloat16)
    in_rows = in_weight.shape[0]
    part_rows = exchange(
        normed, "dp", 0, (dp * req_rows, in_rows), cols_at(in_rows), rows_at(req_rows)
    )
    weight = in_weight.reshape(in_weight.shape[0], 2 * chans)
    terms = jnp.dot(part_rows, weight, preferred_element_type=jnp.float32)
    projected = lax.psum_scatter(
        terms.astype(jnp.bfloat16), "dp", scatter_dimension=0, tiled=True
    ).astype(jnp.float32)
    projected = projected.reshape(req_rows, 2, chans)
    inner_part = projected[:, 0]
    gate_part = projected[:, 1]
    history = conv_state.astype(jnp.float32)
    conv_out = (
        conv_bias
        + conv_weight[3] * inner_part
        + conv_weight[0] * history[0]
        + conv_weight[1] * history[1]
        + conv_weight[2] * history[2]
    )
    activated = jax.nn.silu(conv_out)
    local_inputs = jnp.dot(
        activated.astype(jnp.bfloat16), x_weight, preferred_element_type=jnp.float32
    )
    low = local_inputs.astype(jnp.bfloat16)
    ssm_inputs = jnp.sum(
        exchange(low, "tensor", 1, (n_tensor,) + low.shape, whole_at, block_at).astype(
            jnp.float32
        ),
        0,
    )
    step_low = ssm_inputs[:, :RANK].astype(jnp.bfloat16)
    input_map = ssm_inputs[:, RANK : RANK + NSTATE]
    output_map = ssm_inputs[:, RANK + NSTATE :]
    step_size = jax.nn.softplus(
        jnp.dot(step_low, dt_weight, preferred_element_type=jnp.float32) + dt_bias
    )
    rates = -jnp.exp(a_log)
    gated = scan(
        ssm_state, step_size, activated, gate_part, input_map, output_map, rates, d_skip
    )
    gated_all = gather_pairs(gated, "dp", 9)
    out_cols = jnp.dot(gated_all, out_weight, preferred_element_type=jnp.float32)
    out_chunk = out_weight.shape[1]
    out_terms = exchange(
        out_cols.astype(jnp.bfloat16),
        "dp",
        2,
        (req_rows, dp * out_chunk),
        rows_at(req_rows),
        cols_at(out_chunk),
    )
    mamba_sum = lax.psum_scatter(
        out_terms, "tensor", scatter_dimension=1, tiled=True
    ).astype(jnp.float32)
    residual = (tokens.astype(jnp.float32) + mamba_sum).astype(jnp.bfloat16)
    carried = residual.astype(jnp.float32)
    feat_cols = carried.shape[1]
    gain_slice = lax.dynamic_slice_in_dim(
        moe_gain, lax.axis_index("tensor") * feat_cols, feat_cols, 0
    )
    moe_rows = (carried * gain_slice).astype(jnp.bfloat16)
    capacity = req_rows * lax.axis_size("dp") * TOP // EXPERTS
    limit = jnp.sum(
        (expert_ids[:, :, None] == jnp.arange(EXPERTS, dtype=jnp.int32)[None, None, :])
        * counts[None, None, :],
        -1,
    )
    valid = (expert_ids < EXP_WIN) & (slot_index < limit)
    target = jnp.where(valid, expert_ids * capacity + slot_index, EXP_WIN * capacity)
    part_slots = capacity // dp
    positions = (
        jnp.arange(EXP_WIN * capacity, dtype=jnp.int32)
        .reshape(EXP_WIN, dp, part_slots)
        .transpose(1, 0, 2)
        .reshape(-1)
    )
    slot_match = (positions[:, None] == target[None, :, 0]) | (
        positions[:, None] == target[None, :, 1]
    )
    local_buffer = jnp.dot(
        slot_match.astype(jnp.bfloat16), moe_rows, preferred_element_type=jnp.float32
    ).astype(jnp.bfloat16)
    part_shape = (dp, EXP_WIN * part_slots, feat_cols)
    filled = exchange(
        local_buffer, "dp", 3, part_shape, rows_at(EXP_WIN * part_slots), block_at
    )
    filled = jnp.sum(filled.astype(jnp.float32), 0).astype(jnp.bfloat16)
    per_expert = n_tensor // EXP_WIN
    features = n_tensor * feat_cols
    own_rows = exchange(
        filled,
        "tensor",
        4,
        (part_slots, features),
        lambda i: rows_at(part_slots)(lax.div(i, per_expert)),
        cols_at(feat_cols),
    )
    rows = gather_pairs(own_rows, "dp", 5)
    pre_act = jnp.dot(rows, up_weight, preferred_element_type=jnp.float32)
    hidden = jax.nn.silu(pre_act).astype(jnp.bfloat16)
    partial_out = jnp.dot(hidden, down_weight, preferred_element_type=jnp.float32)
    shares = exchange(
        partial_out.astype(jnp.bfloat16),
        "dp",
        6,
        (dp, part_slots, features),
        rows_at(part_slots),
        block_at,
    )
    shares = jnp.sum(shares.astype(jnp.float32), 0).astype(jnp.bfloat16)
    shares = exchange(
        shares, "tensor", 7, (n_tensor, part_slots, feat_cols), cols_at(feat_cols), block_at
    )
    shares = jnp.sum(
        shares.astype(jnp.float32).reshape(EXP_WIN, per_expert, part_slots, feat_cols), 1
    ).astype(jnp.bfloat16)
    expert_out = gather_pairs(shares.reshape(EXP_WIN * part_slots, feat_cols), "dp", 8).astype(
        jnp.float32
    )
    weights = jnp.where(valid, route_weight, jnp.float32(0.0))
    selector = jnp.where(
        positions[None, :] == target[:, 0:1], weights[:, 0:1], jnp.float32(0.0)
    ) + jnp.where(positions[None, :] == target[:, 1:2], weights[:, 1:2], jnp.float32(0.0))
    moe_sum = jnp.dot(
        selector,
        expert_out.reshape(EXP_WIN * capacity, feat_cols),
        precision=lax.Precision.HIGHEST,
        preferred_element_type=jnp.float32,
    )
    return (carried + moe_sum).astype(jnp.bfloat16)


def solution(mesh):
    placed = (
        P(("groups", "dp"), "tensor"),
        P("dp", None, "tensor"),
        P(None, "tensor"),
        P("tensor"),
        P(None, ("groups", "dp"), "tensor"),
        P("tensor", None),
        P(None, "tensor"),
        P("tensor"),
        P(None, "tensor"),
        P("tensor"),
        P(("groups", "dp"), None, "tensor"),
        P("tensor", "dp"),
        P(),
        P(),
        P(None, ("tensor", "dp")),
        P(("tensor", "dp"), None),
        P(("groups", "dp"), None),
        P(("groups", "dp"), None),
        P("groups"),
        P(("groups", "dp"), None),
    )
    return jax.shard_map(
        shards, mesh=mesh, in_specs=placed, out_specs=P(("groups", "dp"), "tensor"), check_vma=False
    )
```
